32 devices in a mesh: grp: 4 (over y, core), band: 8 (over z, x).
Axes of the slice: x: 2, y: 2, z: 4, core: 2. Of those that a mesh axis runs over, the one named last changes fastest.
Arguments:
- prior_samples: bfloat16 [32, 69, 16, 1024], P('grp', None, 'band'), may hold values from -6 to 6
- conv1_weight: bfloat16 [3, 3, 256, 69], replicated, may hold values from -0.25 to 0.25
- conv1_bias: float32 [256], replicated, may hold values from -3 to 3
- conv2_weight: bfloat16 [3, 3, 69, 256], replicated, may hold values from -0.125 to 0.125
- conv2_bias: float32 [69], replicated, may hold values from -3 to 3
- obs_index: int32 [64, 256], P(('grp', 'band')), may hold values from 0 to 17663
- obs_values: float32 [64, 256], P(('grp', 'band')), may hold values from -6 to 6
- obs_prec: float32 [64, 256], P(('grp', 'band')), may hold values from 0.25 to 4
- neighbours: int32 [64, 8], P(('grp', 'band')), may hold values from 0 to 63
- loc_weight: float32 [64, 8], P(('grp', 'band')), may hold values from 0.2 to 1
Outputs:
- analysis: float32 [32, 69, 16, 1024], P(None, None, 'band', 'grp')
The draws below stay inside these ranges and needn't reach their ends.
Inputs may be any that keep to these rules, and one draw needn't show every extreme that they name: `neighbours`: neighbour patch numbers; a number may repeat or name the patch itself. `obs_index`: observed entry as channel * 256 + column within the patch.
All inputs are finite; a program needn't handle non-finite values.
Results may differ from the reference program's by a relative error of at most 0.0021.
Values may be sent and summed in bfloat16 or wider, within the bound.
A program may use at most 128 MiB of HBM per device.

```python
import math
import jax
import jax.numpy as jnp
from jax import lax

MEMBERS_TOTAL = 32
VARIABLE_TOTAL = 69
HID = 256
TILE_MERIDIANS = 256
NOBS = 256
NBRS = 8
NS_ITERS = 6
PARALLEL_LINES = 16
TILES_ACROSS = 4
LON = 1024
TILE_TOTAL = 64


def set_ends(values, stream_key, least, high):
    place = [jax.random.randint(jax.random.fold_in(stream_key, axis), (), 0, length) for axis, length in enumerate(values.shape)]
    widest = values.shape.index(max(values.shape))
    beside = place[:widest] + [(place[widest] + 1) % values.shape[widest]] + place[widest + 1:]
    return values.at[tuple(place)].set(least).at[tuple(beside)].set(high)


def levels(rng, dims, shards, least, top_value):
    factor_of = 1.0
    for axis_at, blocks in shards:
        heights = jax.random.uniform(jax.random.fold_in(jax.random.fold_in(rng, 6), axis_at), (blocks,), jnp.float32, least / len(shards), top_value / len(shards))
        factor_of = factor_of * jnp.repeat(jnp.exp(heights), dims[axis_at] // blocks).reshape((-1,) + (1,) * (len(dims) - 1 - axis_at))
    return factor_of


def centred(rng, shape, scale, bound, cuts=(), kind=jnp.bfloat16):
    entries = scale * jax.random.normal(rng, shape, jnp.float32)
    if cuts:
        entries = entries * levels(rng, shape, cuts, -0.22, 0.18)
    return jnp.clip(entries, -bound, bound).astype(kind)


def setup_inputs(seed: int = 0) -> dict:
    key_list = jax.random.split(jax.random.key(seed), 11)
    prior_samples = centred(key_list[0], (MEMBERS_TOTAL, VARIABLE_TOTAL, PARALLEL_LINES, LON), 1.0, 6.0, ((0, 4), (2, 8)))
    conv1_weight = centred(key_list[1], (3, 3, HID, VARIABLE_TOTAL), (9 * VARIABLE_TOTAL) ** -0.5, 0.25)
    conv1_bias = centred(key_list[2], (HID,), 0.5, 3.0, (), jnp.float32)
    conv2_weight = centred(key_list[3], (3, 3, VARIABLE_TOTAL, HID), (9 * HID) ** -0.5, 0.125)
    conv2_bias = centred(key_list[4], (VARIABLE_TOTAL,), 0.5, 3.0, (), jnp.float32)
    obs_index = set_ends(jax.random.randint(key_list[5], (TILE_TOTAL, NOBS), 0, VARIABLE_TOTAL * TILE_MERIDIANS), jax.random.fold_in(key_list[5], 1), 0, (VARIABLE_TOTAL * TILE_MERIDIANS) - 1).astype(jnp.int32)
    obs_values = centred(key_list[6], (TILE_TOTAL, NOBS), 1.0, 6.0, ((0, 32),), jnp.float32)
    obs_prec = jnp.clip(jnp.exp(math.log(4.0) - 2.7725887 * jax.random.uniform(key_list[7], (TILE_TOTAL, NOBS), jnp.float32) ** levels(key_list[7], (TILE_TOTAL, NOBS), ((0, 32),), -0.2, 0.2)), 0.25, 4.0)
    neighbours = set_ends(jax.random.randint(key_list[8], (TILE_TOTAL, NBRS), 0, TILE_TOTAL), jax.random.fold_in(key_list[8], 1), 0, TILE_TOTAL - 1).astype(jnp.int32)
    loc_weight = jnp.clip(0.2 + 0.8 * jax.random.uniform(key_list[9], (TILE_TOTAL, NBRS), jnp.float32) ** levels(key_list[9], (TILE_TOTAL, NBRS), ((0, 32),), -0.2, 0.2), 0.2, 1.0)
    return {"prior_samples": prior_samples, "conv1_weight": conv1_weight, "conv1_bias": conv1_bias, "conv2_weight": conv2_weight, "conv2_bias": conv2_bias, "obs_index": obs_index, "obs_values": obs_values, "obs_prec": obs_prec, "neighbours": neighbours, "loc_weight": loc_weight}


def convolve(field, kernel):
    height = field.shape[1]
    padded = jnp.pad(field, ((0, 0), (1, 1), (0, 0)))
    summed = jnp.zeros((kernel.shape[2], height, field.shape[2]), jnp.float32)
    for row_shift in range(3):
        window = padded[:, row_shift:row_shift + height, :]
        for col_shift in range(3):
            shifted = jnp.roll(window, 1 - col_shift, axis=2)
            summed = summed + jnp.einsum('oc,crl->orl', kernel[row_shift, col_shift], shifted)
    return summed

def reference(prior_samples, conv1_weight, conv1_bias, conv2_weight, conv2_bias, obs_index, obs_values, obs_prec, neighbours, loc_weight):
    highest = lax.Precision.HIGHEST
    kernel_one = conv1_weight.astype(jnp.float32)
    kernel_two = conv2_weight.astype(jnp.float32)

    def propagate_realization(member):
        field = member.astype(jnp.float32)
        hidden_fields = jax.nn.silu(convolve(field, kernel_one) + conv1_bias[:, None, None]).astype(jnp.bfloat16)
        hidden_fields = lax.optimization_barrier(hidden_fields).astype(jnp.float32)
        return (field + convolve(hidden_fields, kernel_two) + conv2_bias[:, None, None]).astype(jnp.bfloat16)
    predicted_samples = lax.map(propagate_realization, prior_samples)
    realization_grid = predicted_samples.reshape(MEMBERS_TOTAL, VARIABLE_TOTAL, PARALLEL_LINES, TILES_ACROSS, TILE_MERIDIANS).transpose(3, 2, 0, 1, 4).reshape(TILE_TOTAL, MEMBERS_TOTAL, VARIABLE_TOTAL * TILE_MERIDIANS)
    chosen = jnp.broadcast_to(obs_index[:, None, :], (TILE_TOTAL, MEMBERS_TOTAL, NOBS))
    predicted = jnp.take_along_axis(realization_grid, chosen, axis=2).astype(jnp.float32)
    predicted_mean = lax.optimization_barrier(jnp.mean(predicted, axis=1))
    perturb = predicted - predicted_mean[:, None, :]
    innovation = obs_values - predicted_mean
    gram_local = jnp.einsum('pmo,po,pno->pmn', perturb, obs_prec, perturb, precision=highest)
    pull_vec = jnp.einsum('pmo,po->pm', perturb, obs_prec * innovation, precision=highest)
    identity = jnp.broadcast_to(jnp.eye(MEMBERS_TOTAL, dtype=jnp.float32), (TILE_TOTAL, MEMBERS_TOTAL, MEMBERS_TOTAL))
    matrix = (MEMBERS_TOTAL - 1.0) * identity + gram_local + jnp.einsum('pk,pkmn->pmn', loc_weight, gram_local[neighbours], precision=highest)
    pulled = pull_vec + jnp.einsum('pk,pkm->pm', loc_weight, pull_vec[neighbours], precision=highest)
    norm_scale = jnp.sqrt(lax.optimization_barrier(jnp.sum(matrix * matrix, axis=(1, 2))))
    sqrt_iter = matrix / norm_scale[:, None, None]
    inverse_root = identity
    for sweep in range(NS_ITERS):
        half_step = 1.5 * identity - 0.5 * jnp.einsum('pab,pbc->pac', inverse_root, sqrt_iter, precision=highest)
        sqrt_iter = jnp.einsum('pab,pbc->pac', sqrt_iter, half_step, precision=highest)
        inverse_root = jnp.einsum('pab,pbc->pac', half_step, inverse_root, precision=highest)
    once_applied = jnp.einsum('pab,pb->pa', inverse_root, pulled, precision=highest)
    mean_weight = jnp.einsum('pab,pb->pa', inverse_root, once_applied, precision=highest) / norm_scale[:, None]
    transform = (jnp.sqrt(MEMBERS_TOTAL - 1.0) / jnp.sqrt(norm_scale))[:, None, None] * inverse_root + mean_weight[:, :, None]

    def analyse(pair):
        weight_mat, members = pair
        field = members.astype(jnp.float32)
        centre = lax.optimization_barrier(jnp.mean(field, axis=0))
        spread = field - centre[None, :]
        return centre[None, :] + jnp.einsum('km,kc->mc', weight_mat, spread, precision=highest)
    analysed = lax.map(analyse, (transform, realization_grid))
    return analysed.reshape(TILES_ACROSS, PARALLEL_LINES, MEMBERS_TOTAL, VARIABLE_TOTAL, TILE_MERIDIANS).transpose(2, 3, 1, 0, 4).reshape(MEMBERS_TOTAL, VARIABLE_TOTAL, PARALLEL_LINES, LON)
```

```python
import functools

import jax
import jax.numpy as jnp
from jax import lax
from jax.experimental import pallas as pl
from jax.experimental.pallas import tpu as pltpu
from jax.sharding import PartitionSpec as P

NS_ITERS = 6
PAIR = 2
ROWK = 224
SMEM = pl.BlockSpec(memory_space=pltpu.SMEM)
VMEM = pl.BlockSpec(memory_space=pltpu.VMEM)
HIGH = lax.Precision.HIGHEST


def forecast_kernel(info, own, near, far, w1, b1, w2, b2, *rest, chans, hid, lon, groups):
    outs, (ext, hidden, fore) = rest[:groups], rest[groups:]
    odd, grp = info[0], info[1]
    width = lon // groups

    for member in range(PAIR):
        for source, base in ((own, 2), (near, 4 * (1 - odd)), (far, 4 * odd)):
            for row in range(2):
                x = source[member, row].astype(jnp.float32)
                shifted = [
                    pltpu.roll(x, 1, 1),
                    x,
                    pltpu.roll(x, lon - 1, 1),
                    jnp.zeros((ROWK - 3 * chans, lon), jnp.float32),
                ]
                ext[base + row] = jnp.concatenate(shifted, axis=0).astype(jnp.bfloat16)

        for row in range(4):
            if row == 0:
                keep = info[2]
            elif row == 3:
                keep = info[3]
            else:
                keep = None

            def tile(n, carry, row=row, keep=keep):
                cols = pl.ds(pl.multiple_of(n * 256, 256), 256)
                window = ext[row : row + 3, :, cols].reshape(3 * ROWK, 256)
                h = jnp.dot(w1[...], window, preferred_element_type=jnp.float32) + b1[...]
                h = 0.5 * h
                h = h + h * jnp.tanh(h)
                if keep is not None:
                    h = jnp.where(keep > 0, h, 0.0)
                hidden[row * hid : (row + 1) * hid, cols] = h.astype(jnp.bfloat16)
                return carry

            lax.fori_loop(0, lon // 256, tile, 0, unroll=2)

        for row in range(2):
            summed = jnp.dot(
                w2[...],
                hidden[row * hid : (row + 3) * hid, :],
                preferred_element_type=jnp.float32,
            )
            out = (
                pltpu.roll(summed[:chans], 1, 1)
                + summed[chans : 2 * chans]
                + pltpu.roll(summed[2 * chans :], lon - 1, 1)
                + own[member, row].astype(jnp.float32)
                + b2[...]
            )
            for part in range(groups):
                piece = out[:, part * width : (part + 1) * width]
                fore[part, row, :, member * 8 : (member + 1) * 8, :] = piece.reshape(
                    chans // 8, 8, width
                )

    for step in range(groups):
        for row in range(2):
            block = fore[jnp.bitwise_xor(grp, step), row]
            outs[step][row] = block.reshape(chans * PAIR, width).astype(jnp.bfloat16)


def gram_kernel(info, *rest, pairs, groups, chans, members, nobs, width):
    slabs = rest[: groups * pairs]
    chan, col, obs, prec, field, packed, pred = rest[groups * pairs :]
    grp = info[1]
    blocks = chans // 8
    depth = chans * PAIR
    lane = lax.broadcasted_iota(jnp.int32, (nobs, depth), 1)
    lane_chan = (lane // 16) * 8 + lane % 8
    lane_member = (lane // 8) % 2
    col_iota = lax.broadcasted_iota(jnp.int32, (nobs, width), 1)
    ones = jnp.ones((8, width), jnp.bfloat16)
    packed[...] = jnp.zeros_like(packed)
    for row in range(2):
        pick_chan = lane_chan == chan[:, row : row + 1]
        selects = [
            jnp.where(pick_chan & (lane_member == v), 1.0, 0.0).astype(jnp.bfloat16)
            for v in range(PAIR)
        ]
        pick_col = col_iota == col[:, row : row + 1]
        for step in range(groups):
            source = jnp.bitwise_xor(grp, step)
            for pair in range(pairs):
                slab = slabs[pair * groups + step]
                first = source * (pairs * PAIR) + pair * PAIR
                values = slab[row]
                for block in range(blocks):
                    rows = pl.ds(pl.multiple_of(first * 8, 16), 16)
                    field[row, block, rows, :] = values[block * 16 : (block + 1) * 16, :]
                for v in range(PAIR):
                    g = jnp.dot(selects[v], values, preferred_element_type=jnp.float32)
                    g = jnp.where(pick_col, g, 0.0).astype(jnp.bfloat16)
                    line = lax.dot_general(
                        ones, g, (((1,), (1,)), ((), ())), preferred_element_type=jnp.float32
                    )
                    pred[first + v] = line
        predicted = pred[:, 0, :]
        mean = jnp.sum(predicted, axis=0, keepdims=True) * (1.0 / members)
        perturb = predicted - mean
        innovation = obs[row : row + 1, :] - mean
        both = jnp.concatenate([perturb, jnp.broadcast_to(innovation, (8, nobs))], axis=0)
        packed[:, row * 64 : row * 64 + members + 8] = lax.dot_general(
            perturb * prec[row : row + 1, :],
            both,
            (((1,), (1,)), ((), ())),
            precision=HIGH,
            preferred_element_type=jnp.float32,
        )


def analysis_kernel(neighbours, weights, mine, gathered, field, out, *, members, chans, real, width):
    eye = (
        lax.broadcasted_iota(jnp.int32, (members, members), 0)
        == lax.broadcasted_iota(jnp.int32, (members, members), 1)
    ).astype(jnp.float32)
    wide = members * 8
    expand = (
        lax.broadcasted_iota(jnp.int32, (wide, members), 0) // 8
        == lax.broadcasted_iota(jnp.int32, (wide, members), 1)
    ).astype(jnp.bfloat16)
    same = (
        lax.broadcasted_iota(jnp.int32, (wide, wide), 0) % 8
        == lax.broadcasted_iota(jnp.int32, (wide, wide), 1) % 8
    )

    def dot(a, b):
        return jnp.dot(a, b, precision=HIGH, preferred_element_type=jnp.float32)

    state = []
    for row in range(2):
        total = mine[...] if row == 0 else pltpu.roll(mine[...], 64, 1)
        for k in range(neighbours.shape[1]):
            j = neighbours[row, k]
            gram = gathered[j // 2]
            gram = jnp.where(j % 2 == 1, pltpu.roll(gram, 64, 1), gram)
            total = total + weights[row, k] * gram
        matrix = total[:, :members] + (members - 1.0) * eye
        norm = jnp.sqrt(jnp.sum(matrix * matrix, keepdims=True))
        state.append([matrix / norm, eye, total, norm])
    for sweep in range(NS_ITERS):
        halves = [1.5 * eye - 0.5 * dot(inv, root) for root, inv, _, _ in state]
        for entry, half in zip(state, halves):
            entry[0] = dot(entry[0], half)
            entry[1] = dot(half, entry[1])
    for row in range(2):
        _, inv, total, norm = state[row]
        mean_weight = dot(inv, dot(inv, total))[:, members : members + 1] / norm
        transform = (jnp.sqrt(members - 1.0) / jnp.sqrt(norm)) * inv + mean_weight
        transform = transform + (1.0 - jnp.sum(transform, axis=0, keepdims=True)) * (1.0 / members)
        spread = []
        for piece in range(3):
            part = transform.astype(jnp.bfloat16)
            transform = transform - part.astype(jnp.float32)
            tall = lax.dot_general(
                expand, part, (((1,), (1,)), ((), ())), preferred_element_type=jnp.float32
            ).astype(jnp.bfloat16)
            full = lax.dot_general(
                tall, expand, (((1,), (1,)), ((), ())), preferred_element_type=jnp.float32
            )
            spread.append(jnp.where(same, full, 0.0).astype(jnp.bfloat16))
        for block in range(chans // 8):
            x = field[row, block]
            y = jnp.dot(spread[0], x, preferred_element_type=jnp.float32)
            y = y + jnp.dot(spread[1], x, preferred_element_type=jnp.float32)
            y = y + jnp.dot(spread[2], x, preferred_element_type=jnp.float32)
            count = min(8, real - block * 8)
            for member in range(members):
                for half in range(width // 128):
                    start = (member * real + block * 8) * 4 + half * 2 + row
                    out[pl.ds(start, count, stride=4), :] = y[
                        member * 8 : member * 8 + count, half * 128 : (half + 1) * 128
                    ]


def on_device(
    prior_samples,
    conv1_weight,
    conv1_bias,
    conv2_weight,
    conv2_bias,
    obs_index,
    obs_values,
    obs_prec,
    neighbours,
    loc_weight,
):
    bands = lax.axis_size("band")
    groups = lax.axis_size("grp")
    own_members, real, height, lon = prior_samples.shape
    members = own_members * groups
    hid = conv1_weight.shape[2]
    width = lon // groups
    nobs = obs_index.shape[1]
    chans = -(-real // 8) * 8
    band = lax.axis_index("band")
    grp = lax.axis_index("grp")
    info = jnp.stack([band % 2, grp, band > 0, band < bands - 1]).astype(jnp.int32)

    w1 = jnp.pad(conv1_weight, ((0, 0), (0, 0), (0, 0), (0, chans - real)))
    w1 = jnp.transpose(w1, (2, 0, 1, 3)).reshape(hid, 3, 3 * chans)
    w1 = jnp.pad(w1, ((0, 0), (0, 0), (0, ROWK - 3 * chans))).reshape(hid, 3 * ROWK)
    w2 = jnp.pad(conv2_weight, ((0, 0), (0, 0), (0, chans - real), (0, 0)))
    w2 = jnp.transpose(w2, (1, 2, 0, 3)).reshape(3 * chans, 3 * hid)
    b1 = conv1_bias[:, None]
    b2 = jnp.pad(conv2_bias, (0, chans - real))[:, None]

    swap = [(i, i ^ 1) for i in range(bands)]
    forward = [(i, i - 2) for i in range(3, bands, 2)] + [(i, i + 2) for i in range(0, bands - 2, 2)]
    pairs = own_members // PAIR
    depth = chans * PAIR
    forecast = pl.pallas_call(
        functools.partial(forecast_kernel, chans=chans, hid=hid, lon=lon, groups=groups),
        out_shape=[jax.ShapeDtypeStruct((height, depth, width), jnp.bfloat16)] * groups,
        in_specs=[SMEM] + [VMEM] * 7,
        out_specs=[VMEM] * groups,
        scratch_shapes=[
            pltpu.VMEM((6, ROWK, lon), jnp.bfloat16),
            pltpu.VMEM((4 * hid, lon), jnp.bfloat16),
            pltpu.VMEM((groups, height, chans // 8, 8 * PAIR, width), jnp.float32),
        ],
        compiler_params=pltpu.CompilerParams(vmem_limit_bytes=40 * 2**20),
        cost_estimate=pl.CostEstimate(
            flops=2 * PAIR * 6 * hid * 768 * lon, bytes_accessed=4 * 2**20, transcendentals=0
        ),
        name="forecast",
    )
    slabs = []
    for pair in range(pairs):
        own = prior_samples[pair * PAIR : (pair + 1) * PAIR]
        own = jnp.pad(jnp.transpose(own, (0, 2, 1, 3)), ((0, 0), (0, 0), (0, chans - real), (0, 0)))
        near = lax.ppermute(own, "band", swap)
        far = lax.ppermute(near, "band", forward)
        pieces = forecast(info, own, near, far, w1, b1, w2, b2)
        for step in range(groups):
            piece = pieces[step]
            if step:
                piece = lax.ppermute(piece, "grp", [(i, i ^ step) for i in range(groups)])
            slabs.append(piece)

    chan = (obs_index // width).T
    col = (obs_index % width).T
    field, packed = pl.pallas_call(
        functools.partial(
            gram_kernel,
            pairs=pairs,
            groups=groups,
            chans=chans,
            members=members,
            nobs=nobs,
            width=width,
        ),
        out_shape=[
            jax.ShapeDtypeStruct((height, chans // 8, members * 8, width), jnp.bfloat16),
            jax.ShapeDtypeStruct((members, 128), jnp.float32),
        ],
        in_specs=[SMEM] + [VMEM] * (len(slabs) + 4),
        out_specs=[VMEM] * 2,
        scratch_shapes=[pltpu.VMEM((members, 8, nobs), jnp.float32)],
        compiler_params=pltpu.CompilerParams(vmem_limit_bytes=40 * 2**20),
        name="grams",
    )(info, *slabs, chan, col, obs_values, obs_prec)
    gathered = lax.all_gather(packed, ("grp", "band"), axis=0)
    out = pl.pallas_call(
        functools.partial(analysis_kernel, members=members, chans=chans, real=real, width=width),
        out_shape=jax.ShapeDtypeStruct((members * real * 2 * height, 128), jnp.float32),
        in_specs=[SMEM, SMEM, VMEM, VMEM, VMEM],
        out_specs=VMEM,
        compiler_params=pltpu.CompilerParams(vmem_limit_bytes=40 * 2**20),
        name="analyse",
    )(neighbours, loc_weight, packed, gathered, field)
    out = out.reshape(members, real, width // 128, height, 128)
    return jnp.transpose(out, (0, 1, 3, 2, 4)).reshape(members, real, height, width)


def solution(mesh):
    placed = (
        P("grp", None, "band", None),
        P(),
        P(),
        P(),
        P(),
        P(("grp", "band"), None),
        P(("grp", "band"), None),
        P(("grp", "band"), None),
        P(("grp", "band"), None),
        P(("grp", "band"), None),
    )
    return jax.shard_map(
        on_device,
        mesh=mesh,
        in_specs=placed,
        out_specs=P(None, None, "band", "grp"),
        check_vma=False,
    )
```

```python
import functools

import jax
import jax.numpy as jnp
from jax import lax
from jax.experimental import pallas as pl
from jax.experimental.pallas import tpu as pltpu
from jax.sharding import PartitionSpec as P

NS_ITERS = 6
PAIR = 2
ROWK = 224
SMEM = pl.BlockSpec(memory_space=pltpu.SMEM)
VMEM = pl.BlockSpec(memory_space=pltpu.VMEM)
MESH = pl.DeviceIdType.MESH
HIGH = lax.Precision.HIGHEST


def forecast_kernel(info, own, near, far, w1, b1, w2, b2, *rest, chans, hid, lon, groups):
    outs, (ext, hidden, fore) = rest[:groups], rest[groups:]
    odd, grp = info[0], info[1]
    width = lon // groups

    for member in range(PAIR):
        for source, base in ((own, 2), (near, 4 * (1 - odd)), (far, 4 * odd)):
            for row in range(2):
                x = source[member, row].astype(jnp.float32)
                shifted = [
                    pltpu.roll(x, 1, 1),
                    x,
                    pltpu.roll(x, lon - 1, 1),
                    jnp.zeros((ROWK - 3 * chans, lon), jnp.float32),
                ]
                ext[base + row] = jnp.concatenate(shifted, axis=0).astype(jnp.bfloat16)

        for row in range(4):
            if row == 0:
                keep = info[2]
            elif row == 3:
                keep = info[3]
            else:
                keep = None

            def tile(n, carry, row=row, keep=keep):
                cols = pl.ds(pl.multiple_of(n * 256, 256), 256)
                window = ext[row : row + 3, :, cols].reshape(3 * ROWK, 256)
                h = jnp.dot(w1[...], window, preferred_element_type=jnp.float32) + b1[...]
                h = 0.5 * h
                h = h + h * jnp.tanh(h)
                if keep is not None:
                    h = jnp.where(keep > 0, h, 0.0)
                hidden[row * hid : (row + 1) * hid, cols] = h.astype(jnp.bfloat16)
                return carry

            lax.fori_loop(0, lon // 256, tile, 0, unroll=2)

        for row in range(2):
            summed = jnp.dot(
                w2[...],
                hidden[row * hid : (row + 3) * hid, :],
                preferred_element_type=jnp.float32,
            )
            out = (
                pltpu.roll(summed[:chans], 1, 1)
                + summed[chans : 2 * chans]
                + pltpu.roll(summed[2 * chans :], lon - 1, 1)
                + own[member, row].astype(jnp.float32)
                + b2[...]
            )
            for part in range(groups):
                piece = out[:, part * width : (part + 1) * width]
                fore[part, row, :, member * 8 : (member + 1) * 8, :] = piece.reshape(
                    chans // 8, 8, width
                )

    for step in range(groups):
        for row in range(2):
            block = fore[jnp.bitwise_xor(grp, step), row]
            outs[step][row] = block.reshape(chans * PAIR, width).astype(jnp.bfloat16)


def exchange_start(bands, groups):
    grp, band = lax.axis_index("grp"), lax.axis_index("band")
    barrier = pltpu.get_barrier_semaphore()
    for step in range(1, bands):
        peer = lax.rem(band + step, bands)
        pl.semaphore_signal(barrier, inc=1, device_id={"band": peer}, device_id_type=MESH)
    for step in range(1, groups):
        peer = jnp.bitwise_xor(grp, step)
        pl.semaphore_signal(barrier, inc=1, device_id={"grp": peer}, device_id_type=MESH)


def exchange_all(gathered, bands, groups, band_sems, grp_sems):
    grp, band = lax.axis_index("grp"), lax.axis_index("band")
    pl.semaphore_wait(pltpu.get_barrier_semaphore(), bands + groups - 2)
    first = [
        pltpu.make_async_remote_copy(
            src_ref=gathered.at[grp, band],
            dst_ref=gathered.at[grp, band],
            send_sem=band_sems.at[0, step],
            recv_sem=band_sems.at[1, step],
            device_id={"band": lax.rem(band + step, bands)},
            device_id_type=MESH,
        )
        for step in range(1, bands)
    ]
    for copy in first:
        copy.start()
    for copy in first:
        copy.wait()
    second = [
        pltpu.make_async_remote_copy(
            src_ref=gathered.at[grp],
            dst_ref=gathered.at[grp],
            send_sem=grp_sems.at[0, step],
            recv_sem=grp_sems.at[1, step],
            device_id={"grp": jnp.bitwise_xor(grp, step)},
            device_id_type=MESH,
        )
        for step in range(1, groups)
    ]
    for copy in second:
        copy.start()
    for copy in second:
        copy.wait()


def gram_kernel(*rest, pairs, bands, groups, chans, members, nobs, width):
    slabs = rest[: groups * pairs]
    chan, col, obs, prec, field, packed, gathered, pred, band_sems, grp_sems = rest[groups * pairs :]
    exchange_start(bands, groups)
    grp = lax.axis_index("grp")
    blocks = chans // 8
    depth = chans * PAIR
    lane = lax.broadcasted_iota(jnp.int32, (nobs, depth), 1)
    lane_chan = (lane // 16) * 8 + lane % 8
    lane_member = (lane // 8) % 2
    col_iota = lax.broadcasted_iota(jnp.int32, (nobs, width), 1)
    ones = jnp.ones((8, width), jnp.bfloat16)
    packed[...] = jnp.zeros_like(packed)
    for row in range(2):
        pick_chan = lane_chan == chan[:, row : row + 1]
        selects = [
            jnp.where(pick_chan & (lane_member == v), 1.0, 0.0).astype(jnp.bfloat16)
            for v in range(PAIR)
        ]
        pick_col = col_iota == col[:, row : row + 1]
        for step in range(groups):
            source = jnp.bitwise_xor(grp, step)
            for pair in range(pairs):
                slab = slabs[pair * groups + step]
                first = source * (pairs * PAIR) + pair * PAIR
                values = slab[row]
                for block in range(blocks):
                    rows = pl.ds(pl.multiple_of(first * 8, 16), 16)
                    field[row, block, rows, :] = values[block * 16 : (block + 1) * 16, :]
                for v in range(PAIR):
                    g = jnp.dot(selects[v], values, preferred_element_type=jnp.float32)
                    g = jnp.where(pick_col, g, 0.0).astype(jnp.bfloat16)
                    line = lax.dot_general(
                        ones, g, (((1,), (1,)), ((), ())), preferred_element_type=jnp.float32
                    )
                    pred[first + v] = line
        predicted = pred[:, 0, :]
        mean = jnp.sum(predicted, axis=0, keepdims=True) * (1.0 / members)
        perturb = predicted - mean
        innovation = obs[row : row + 1, :] - mean
        both = jnp.concatenate([perturb, jnp.broadcast_to(innovation, (8, nobs))], axis=0)
        packed[:, row * 64 : row * 64 + members + 8] = lax.dot_general(
            perturb * prec[row : row + 1, :],
            both,
            (((1,), (1,)), ((), ())),
            precision=HIGH,
            preferred_element_type=jnp.float32,
        )
    gathered[grp, lax.axis_index("band")] = packed[...]
    exchange_all(gathered, bands, groups, band_sems, grp_sems)


def analysis_kernel(neighbours, weights, mine, gathered, field, out, *, members, chans, real, width):
    eye = (
        lax.broadcasted_iota(jnp.int32, (members, members), 0)
        == lax.broadcasted_iota(jnp.int32, (members, members), 1)
    ).astype(jnp.float32)
    wide = members * 8
    expand = (
        lax.broadcasted_iota(jnp.int32, (wide, members), 0) // 8
        == lax.broadcasted_iota(jnp.int32, (wide, members), 1)
    ).astype(jnp.bfloat16)
    same = (
        lax.broadcasted_iota(jnp.int32, (wide, wide), 0) % 8
        == lax.broadcasted_iota(jnp.int32, (wide, wide), 1) % 8
    )

    def dot(a, b):
        return jnp.dot(a, b, precision=HIGH, preferred_element_type=jnp.float32)

    state = []
    for row in range(2):
        total = mine[...] if row == 0 else pltpu.roll(mine[...], 64, 1)
        for k in range(neighbours.shape[1]):
            j = neighbours[row, k]
            bands = gathered.shape[1]
            gram = gathered[j // (2 * bands), (j // 2) % bands]
            gram = jnp.where(j % 2 == 1, pltpu.roll(gram, 64, 1), gram)
            total = total + weights[row, k] * gram
        matrix = total[:, :members] + (members - 1.0) * eye
        norm = jnp.sqrt(jnp.sum(matrix * matrix, keepdims=True))
        state.append([matrix / norm, eye, total, norm])
    for sweep in range(NS_ITERS):
        halves = [1.5 * eye - 0.5 * dot(inv, root) for root, inv, _, _ in state]
        for entry, half in zip(state, halves):
            entry[0] = dot(entry[0], half)
            entry[1] = dot(half, entry[1])
    for row in range(2):
        _, inv, total, norm = state[row]
        mean_weight = dot(inv, dot(inv, total))[:, members : members + 1] / norm
        transform = (jnp.sqrt(members - 1.0) / jnp.sqrt(norm)) * inv + mean_weight
        transform = transform + (1.0 - jnp.sum(transform, axis=0, keepdims=True)) * (1.0 / members)
        spread = []
        for piece in range(3):
            part = transform.astype(jnp.bfloat16)
            transform = transform - part.astype(jnp.float32)
            tall = lax.dot_general(
                expand, part, (((1,), (1,)), ((), ())), preferred_element_type=jnp.float32
            ).astype(jnp.bfloat16)
            full = lax.dot_general(
                tall, expand, (((1,), (1,)), ((), ())), preferred_element_type=jnp.float32
            )
            spread.append(jnp.where(same, full, 0.0).astype(jnp.bfloat16))
        for block in range(chans // 8):
            x = field[row, block]
            y = jnp.dot(spread[0], x, preferred_element_type=jnp.float32)
            y = y + jnp.dot(spread[1], x, preferred_element_type=jnp.float32)
            y = y + jnp.dot(spread[2], x, preferred_element_type=jnp.float32)
            count = min(8, real - block * 8)
            for member in range(members):
                for half in range(width // 128):
                    start = (member * real + block * 8) * 4 + half * 2 + row
                    out[pl.ds(start, count, stride=4), :] = y[
                        member * 8 : member * 8 + count, half * 128 : (half + 1) * 128
                    ]


def on_device(
    prior_samples,
    conv1_weight,
    conv1_bias,
    conv2_weight,
    conv2_bias,
    obs_index,
    obs_values,
    obs_prec,
    neighbours,
    loc_weight,
):
    bands = lax.axis_size("band")
    groups = lax.axis_size("grp")
    own_members, real, height, lon = prior_samples.shape
    members = own_members * groups
    hid = conv1_weight.shape[2]
    width = lon // groups
    nobs = obs_index.shape[1]
    chans = -(-real // 8) * 8
    band = lax.axis_index("band")
    grp = lax.axis_index("grp")
    info = jnp.stack([band % 2, grp, band > 0, band < bands - 1]).astype(jnp.int32)

    w1 = jnp.pad(conv1_weight, ((0, 0), (0, 0), (0, 0), (0, chans - real)))
    w1 = jnp.transpose(w1, (2, 0, 1, 3)).reshape(hid, 3, 3 * chans)
    w1 = jnp.pad(w1, ((0, 0), (0, 0), (0, ROWK - 3 * chans))).reshape(hid, 3 * ROWK)
    w2 = jnp.pad(conv2_weight, ((0, 0), (0, 0), (0, chans - real), (0, 0)))
    w2 = jnp.transpose(w2, (1, 2, 0, 3)).reshape(3 * chans, 3 * hid)
    b1 = conv1_bias[:, None]
    b2 = jnp.pad(conv2_bias, (0, chans - real))[:, None]

    swap = [(i, i ^ 1) for i in range(bands)]
    forward = [(i, i - 2) for i in range(3, bands, 2)] + [(i, i + 2) for i in range(0, bands - 2, 2)]
    pairs = own_members // PAIR
    depth = chans * PAIR
    forecast = pl.pallas_call(
        functools.partial(forecast_kernel, chans=chans, hid=hid, lon=lon, groups=groups),
        out_shape=[jax.ShapeDtypeStruct((height, depth, width), jnp.bfloat16)] * groups,
        in_specs=[SMEM] + [VMEM] * 7,
        out_specs=[VMEM] * groups,
        scratch_shapes=[
            pltpu.VMEM((6, ROWK, lon), jnp.bfloat16),
            pltpu.VMEM((4 * hid, lon), jnp.bfloat16),
            pltpu.VMEM((groups, height, chans // 8, 8 * PAIR, width), jnp.float32),
        ],
        compiler_params=pltpu.CompilerParams(vmem_limit_bytes=40 * 2**20),
        cost_estimate=pl.CostEstimate(
            flops=2 * PAIR * 6 * hid * 768 * lon, bytes_accessed=4 * 2**20, transcendentals=0
        ),
        name="forecast",
    )
    slabs = []
    for pair in range(pairs):
        own = prior_samples[pair * PAIR : (pair + 1) * PAIR]
        own = jnp.pad(jnp.transpose(own, (0, 2, 1, 3)), ((0, 0), (0, 0), (0, chans - real), (0, 0)))
        near = lax.ppermute(own, "band", swap)
        if pair >= 2:
            near, _ = lax.optimization_barrier((near, slabs[(pair - 2) * groups]))
        far = lax.ppermute(near, "band", forward)
        pieces = forecast(info, own, near, far, w1, b1, w2, b2)
        for step in range(groups):
            piece = pieces[step]
            if step:
                piece = lax.ppermute(piece, "grp", [(i, i ^ step) for i in range(groups)])
            slabs.append(piece)

    chan = (obs_index // width).T
    col = (obs_index % width).T
    field, packed, gathered = pl.pallas_call(
        functools.partial(
            gram_kernel,
            pairs=pairs,
            bands=bands,
            groups=groups,
            chans=chans,
            members=members,
            nobs=nobs,
            width=width,
        ),
        out_shape=[
            jax.ShapeDtypeStruct((height, chans // 8, members * 8, width), jnp.bfloat16),
            jax.ShapeDtypeStruct((members, 128), jnp.float32),
            jax.ShapeDtypeStruct((groups, bands, members, 128), jnp.float32),
        ],
        in_specs=[VMEM] * (len(slabs) + 4),
        out_specs=[VMEM] * 3,
        scratch_shapes=[
            pltpu.VMEM((members, 8, nobs), jnp.float32),
            pltpu.SemaphoreType.DMA((2, bands)),
            pltpu.SemaphoreType.DMA((2, groups)),
        ],
        compiler_params=pltpu.CompilerParams(
            vmem_limit_bytes=40 * 2**20, collective_id=1, has_side_effects=True
        ),
        name="grams",
    )(*slabs, chan, col, obs_values, obs_prec)
    out = pl.pallas_call(
        functools.partial(analysis_kernel, members=members, chans=chans, real=real, width=width),
        out_shape=jax.ShapeDtypeStruct((members * real * 2 * height, 128), jnp.float32),
        in_specs=[SMEM, SMEM, VMEM, VMEM, VMEM],
        out_specs=VMEM,
        compiler_params=pltpu.CompilerParams(vmem_limit_bytes=40 * 2**20),
        name="analyse",
    )(neighbours, loc_weight, packed, gathered, field)
    out = out.reshape(members, real, width // 128, height, 128)
    return jnp.transpose(out, (0, 1, 3, 2, 4)).reshape(members, real, height, width)


def solution(mesh):
    placed = (
        P("grp", None, "band", None),
        P(),
        P(),
        P(),
        P(),
        P(("grp", "band"), None),
        P(("grp", "band"), None),
        P(("grp", "band"), None),
        P(("grp", "band"), None),
        P(("grp", "band"), None),
    )
    return jax.shard_map(
        on_device,
        mesh=mesh,
        in_specs=placed,
        out_specs=P(None, None, "band", "grp"),
        check_vma=False,
    )
```

```python
import functools

import jax
import jax.numpy as jnp
from jax import lax
from jax.experimental import pallas as pl
from jax.experimental.pallas import tpu as pltpu
from jax.sharding import PartitionSpec as P

NS_ITERS = 6
PAIR = 2
AHEAD = 3
ROWK = 224
SMEM = pl.BlockSpec(memory_space=pltpu.SMEM)
VMEM = pl.BlockSpec(memory_space=pltpu.VMEM)
MESH = pl.DeviceIdType.MESH
HIGH = lax.Precision.HIGHEST


def forecast_kernel(
    own, w1, b1, w2, b2, field, near, far, ext, hidden, fore, stage, swap_sems, pass_sems, part_sems,
    *, chans, hid, lon, groups, bands
):
    grp, band = lax.axis_index("grp"), lax.axis_index("band")
    odd = lax.rem(band, 2)
    count = own.shape[0]
    width = lon // groups
    partner = band + 1 - 2 * odd
    target = band + 2 - 4 * odd
    origin = band - 2 + 4 * odd
    sends = (target >= 0) & (target < bands)
    receives = (origin >= 0) & (origin < bands)
    barrier = pltpu.get_barrier_semaphore()

    def greet(axis, peer):
        pl.semaphore_signal(barrier, inc=1, device_id={axis: peer}, device_id_type=MESH)

    greet("band", partner)
    for step in range(1, groups):
        greet("grp", jnp.bitwise_xor(grp, step))
    pl.when(receives)(lambda: greet("band", origin))

    @pl.when(jnp.logical_not(receives))
    def _():
        far[...] = jnp.zeros_like(far)

    pl.semaphore_wait(barrier, groups + sends.astype(jnp.int32))

    def swap(m):
        return pltpu.make_async_remote_copy(
            src_ref=own.at[m],
            dst_ref=near.at[m],
            send_sem=swap_sems.at[0, m],
            recv_sem=swap_sems.at[1, m],
            device_id={"band": partner},
            device_id_type=MESH,
        )

    def onward(m):
        return pltpu.make_async_remote_copy(
            src_ref=near.at[m],
            dst_ref=far.at[m],
            send_sem=pass_sems.at[0, m],
            recv_sem=pass_sems.at[1, m],
            device_id={"band": target},
            device_id_type=MESH,
        )

    def handout(pair, step):
        rows = pl.ds(pl.multiple_of((grp * count + pair * PAIR) * 8, 16), 8 * PAIR)
        return pltpu.make_async_remote_copy(
            src_ref=stage.at[pair, step],
            dst_ref=field.at[:, :, rows, :],
            send_sem=part_sems.at[0, pair, step],
            recv_sem=part_sems.at[1, pair, step],
            device_id={"grp": jnp.bitwise_xor(grp, step)},
            device_id_type=MESH,
        )

    for m in range(AHEAD):
        swap(m).start()
    swap(0).wait_recv()
    pl.when(sends)(lambda: onward(0).start())

    def one(pair, member):
        m = pair * PAIR + member

        @pl.when(m + 1 < count)
        def _():
            swap(m + 1).wait_recv()
            pl.when(sends)(lambda: onward(m + 1).start())

        @pl.when(m + AHEAD < count)
        def _():
            swap(m + AHEAD).start()

        pl.when(receives)(lambda: onward(m).wait_recv())

        for source, base in ((own, 2), (near, 4 * (1 - odd)), (far, 4 * odd)):
            for row in range(2):
                x = source[m, row].astype(jnp.float32)
                shifted = [
                    pltpu.roll(x, 1, 1),
                    x,
                    pltpu.roll(x, lon - 1, 1),
                    jnp.zeros((ROWK - 3 * chans, lon), jnp.float32),
                ]
                ext[base + row] = jnp.concatenate(shifted, axis=0).astype(jnp.bfloat16)

        for row in range(4):
            if row == 0:
                keep = band > 0
            elif row == 3:
                keep = band < bands - 1
            else:
                keep = None

            def tile(n, carry, row=row, keep=keep):
                cols = pl.ds(pl.multiple_of(n * 256, 256), 256)
                window = ext[row : row + 3, :, cols].reshape(3 * ROWK, 256)
                h = jnp.dot(w1[...], window, preferred_element_type=jnp.float32) + b1[...]
                h = 0.5 * h
                h = h + h * jnp.tanh(h)
                if keep is not None:
                    h = jnp.where(keep, h, 0.0)
                hidden[row * hid : (row + 1) * hid, cols] = h.astype(jnp.bfloat16)
                return carry

            lax.fori_loop(0, lon // 256, tile, 0, unroll=2)

        for row in range(2):
            summed = jnp.dot(
                w2[...],
                hidden[row * hid : (row + 3) * hid, :],
                preferred_element_type=jnp.float32,
            )
            out = (
                pltpu.roll(summed[:chans], 1, 1)
                + summed[chans : 2 * chans]
                + pltpu.roll(summed[2 * chans :], lon - 1, 1)
                + own[m, row].astype(jnp.float32)
                + b2[...]
            )
            for part in range(groups):
                piece = out[:, part * width : (part + 1) * width]
                fore[part, row, :, member * 8 : (member + 1) * 8, :] = piece.reshape(
                    chans // 8, 8, width
                )

    def both(pair, carry):
        for member in range(PAIR):
            one(pair, member)
        rows = pl.ds(pl.multiple_of((grp * count + pair * PAIR) * 8, 16), 8 * PAIR)
        for row in range(2):
            field[row, :, rows, :] = fore[grp, row].astype(jnp.bfloat16)
            for step in range(1, groups):
                stage[pair, step, row] = fore[jnp.bitwise_xor(grp, step), row].astype(jnp.bfloat16)
        for step in range(1, groups):
            handout(pair, step).start()
        return carry

    lax.fori_loop(0, count // PAIR, both, 0)

    def finish(pair, carry):
        for step in range(1, groups):
            handout(pair, step).wait()
        for member in range(PAIR):
            m = pair * PAIR + member
            swap(m).wait_send()
            pl.when(sends)(lambda m=m: onward(m).wait_send())
        return carry

    lax.fori_loop(0, count // PAIR, finish, 0)


def exchange_start(bands, groups):
    grp, band = lax.axis_index("grp"), lax.axis_index("band")
    barrier = pltpu.get_barrier_semaphore()
    for step in range(1, bands):
        peer = lax.rem(band + step, bands)
        pl.semaphore_signal(barrier, inc=1, device_id={"band": peer}, device_id_type=MESH)
    for step in range(1, groups):
        peer = jnp.bitwise_xor(grp, step)
        pl.semaphore_signal(barrier, inc=1, device_id={"grp": peer}, device_id_type=MESH)


def exchange_all(gathered, bands, groups, band_sems, grp_sems):
    grp, band = lax.axis_index("grp"), lax.axis_index("band")
    pl.semaphore_wait(pltpu.get_barrier_semaphore(), bands + groups - 2)
    first = [
        pltpu.make_async_remote_copy(
            src_ref=gathered.at[grp, band],
            dst_ref=gathered.at[grp, band],
            send_sem=band_sems.at[0, step],
            recv_sem=band_sems.at[1, step],
            device_id={"band": lax.rem(band + step, bands)},
            device_id_type=MESH,
        )
        for step in range(1, bands)
    ]
    for copy in first:
        copy.start()
    for copy in first:
        copy.wait()
    second = [
        pltpu.make_async_remote_copy(
            src_ref=gathered.at[grp],
            dst_ref=gathered.at[grp],
            send_sem=grp_sems.at[0, step],
            recv_sem=grp_sems.at[1, step],
            device_id={"grp": jnp.bitwise_xor(grp, step)},
            device_id_type=MESH,
        )
        for step in range(1, groups)
    ]
    for copy in second:
        copy.start()
    for copy in second:
        copy.wait()


def gram_kernel(
    field, chan, col, obs, prec, packed, gathered, pred, band_sems, grp_sems,
    *, bands, groups, chans, members, nobs, width
):
    exchange_start(bands, groups)
    grp = lax.axis_index("grp")
    depth = chans * PAIR
    lane = lax.broadcasted_iota(jnp.int32, (nobs, depth), 1)
    lane_chan = (lane // 16) * 8 + lane % 8
    lane_member = (lane // 8) % 2
    col_iota = lax.broadcasted_iota(jnp.int32, (nobs, width), 1)
    ones = jnp.ones((8, width), jnp.bfloat16)
    packed[...] = jnp.zeros_like(packed)
    for row in range(2):
        pick_chan = lane_chan == chan[:, row : row + 1]
        selects = [
            jnp.where(pick_chan & (lane_member == v), 1.0, 0.0).astype(jnp.bfloat16)
            for v in range(PAIR)
        ]
        pick_col = col_iota == col[:, row : row + 1]

        for first in range(0, members, PAIR):
            values = field[row, :, first * 8 : (first + PAIR) * 8, :].reshape(depth, width)
            for v in range(PAIR):
                g = jnp.dot(selects[v], values, preferred_element_type=jnp.float32)
                g = jnp.where(pick_col, g, 0.0).astype(jnp.bfloat16)
                line = lax.dot_general(
                    ones, g, (((1,), (1,)), ((), ())), preferred_element_type=jnp.float32
                )
                pred[first + v] = line
        predicted = pred[:, 0, :]
        mean = jnp.sum(predicted, axis=0, keepdims=True) * (1.0 / members)
        perturb = predicted - mean
        innovation = obs[row : row + 1, :] - mean
        both = jnp.concatenate([perturb, jnp.broadcast_to(innovation, (8, nobs))], axis=0)
        packed[:, row * 64 : row * 64 + members + 8] = lax.dot_general(
            perturb * prec[row : row + 1, :],
            both,
            (((1,), (1,)), ((), ())),
            precision=HIGH,
            preferred_element_type=jnp.float32,
        )
    gathered[grp, lax.axis_index("band")] = packed[...]
    exchange_all(gathered, bands, groups, band_sems, grp_sems)


def analysis_kernel(neighbours, weights, mine, gathered, field, out, *, members, chans, real, width):
    eye = (
        lax.broadcasted_iota(jnp.int32, (members, members), 0)
        == lax.broadcasted_iota(jnp.int32, (members, members), 1)
    ).astype(jnp.float32)
    wide = members * 8
    expand = (
        lax.broadcasted_iota(jnp.int32, (wide, members), 0) // 8
        == lax.broadcasted_iota(jnp.int32, (wide, members), 1)
    ).astype(jnp.bfloat16)
    same = (
        lax.broadcasted_iota(jnp.int32, (wide, wide), 0) % 8
        == lax.broadcasted_iota(jnp.int32, (wide, wide), 1) % 8
    )

    def dot(a, b):
        return jnp.dot(a, b, precision=HIGH, preferred_element_type=jnp.float32)

    state = []
    for row in range(2):
        total = mine[...] if row == 0 else pltpu.roll(mine[...], 64, 1)
        for k in range(neighbours.shape[1]):
            j = neighbours[row, k]
            bands = gathered.shape[1]
            gram = gathered[j // (2 * bands), (j // 2) % bands]
            gram = jnp.where(j % 2 == 1, pltpu.roll(gram, 64, 1), gram)
            total = total + weights[row, k] * gram
        matrix = total[:, :members] + (members - 1.0) * eye
        norm = jnp.sqrt(jnp.sum(matrix * matrix, keepdims=True))
        state.append([matrix / norm, eye, total, norm])
    for sweep in range(NS_ITERS):
        halves = [1.5 * eye - 0.5 * dot(inv, root) for root, inv, _, _ in state]
        for entry, half in zip(state, halves):
            entry[0] = dot(entry[0], half)
            entry[1] = dot(half, entry[1])
    for row in range(2):
        _, inv, total, norm = state[row]
        mean_weight = dot(inv, dot(inv, total))[:, members : members + 1] / norm
        transform = (jnp.sqrt(members - 1.0) / jnp.sqrt(norm)) * inv + mean_weight
        transform = transform + (1.0 - jnp.sum(transform, axis=0, keepdims=True)) * (1.0 / members)
        spread = []
        for piece in range(3):
            part = transform.astype(jnp.bfloat16)
            transform = transform - part.astype(jnp.float32)
            tall = lax.dot_general(
                expand, part, (((1,), (1,)), ((), ())), preferred_element_type=jnp.float32
            ).astype(jnp.bfloat16)
            full = lax.dot_general(
                tall, expand, (((1,), (1,)), ((), ())), preferred_element_type=jnp.float32
            )
            spread.append(jnp.where(same, full, 0.0).astype(jnp.bfloat16))
        for block in range(chans // 8):
            x = field[row, block]
            y = jnp.dot(spread[0], x, preferred_element_type=jnp.float32)
            y = y + jnp.dot(spread[1], x, preferred_element_type=jnp.float32)
            y = y + jnp.dot(spread[2], x, preferred_element_type=jnp.float32)
            count = min(8, real - block * 8)
            for member in range(members):
                for half in range(width // 128):
                    start = (member * real + block * 8) * 4 + half * 2 + row
                    out[pl.ds(start, count, stride=4), :] = y[
                        member * 8 : member * 8 + count, half * 128 : (half + 1) * 128
                    ]


def on_device(
    prior_samples,
    conv1_weight,
    conv1_bias,
    conv2_weight,
    conv2_bias,
    obs_index,
    obs_values,
    obs_prec,
    neighbours,
    loc_weight,
):
    bands = lax.axis_size("band")
    groups = lax.axis_size("grp")
    own_members, real, height, lon = prior_samples.shape
    members = own_members * groups
    hid = conv1_weight.shape[2]
    width = lon // groups
    nobs = obs_index.shape[1]
    chans = -(-real // 8) * 8

    w1 = jnp.pad(conv1_weight, ((0, 0), (0, 0), (0, 0), (0, chans - real)))
    w1 = jnp.transpose(w1, (2, 0, 1, 3)).reshape(hid, 3, 3 * chans)
    w1 = jnp.pad(w1, ((0, 0), (0, 0), (0, ROWK - 3 * chans))).reshape(hid, 3 * ROWK)
    w2 = jnp.pad(conv2_weight, ((0, 0), (0, 0), (0, chans - real), (0, 0)))
    w2 = jnp.transpose(w2, (1, 2, 0, 3)).reshape(3 * chans, 3 * hid)
    b1 = conv1_bias[:, None]
    b2 = jnp.pad(conv2_bias, (0, chans - real))[:, None]

    pairs = own_members // PAIR
    blocks = chans // 8
    own = jnp.transpose(prior_samples, (0, 2, 1, 3))
    own = jnp.pad(own, ((0, 0), (0, 0), (0, chans - real), (0, 0)))
    halo = pltpu.VMEM((own_members, height, chans, lon), jnp.bfloat16)
    field = pl.pallas_call(
        functools.partial(
            forecast_kernel, chans=chans, hid=hid, lon=lon, groups=groups, bands=bands
        ),
        out_shape=jax.ShapeDtypeStruct((height, blocks, members * 8, width), jnp.bfloat16),
        in_specs=[VMEM] * 5,
        out_specs=VMEM,
        scratch_shapes=[
            halo,
            halo,
            pltpu.VMEM((6, ROWK, lon), jnp.bfloat16),
            pltpu.VMEM((4 * hid, lon), jnp.bfloat16),
            pltpu.VMEM((groups, height, blocks, 8 * PAIR, width), jnp.float32),
            pltpu.VMEM((pairs, groups, height, blocks, 8 * PAIR, width), jnp.bfloat16),
            pltpu.SemaphoreType.DMA((2, own_members)),
            pltpu.SemaphoreType.DMA((2, own_members)),
            pltpu.SemaphoreType.DMA((2, pairs, groups)),
        ],
        compiler_params=pltpu.CompilerParams(
            vmem_limit_bytes=44 * 2**20, collective_id=2, has_side_effects=True
        ),
        name="forecast",
    )(own, w1, b1, w2, b2)

    chan = (obs_index // width).T
    col = (obs_index % width).T
    packed, gathered = pl.pallas_call(
        functools.partial(
            gram_kernel,
            bands=bands,
            groups=groups,
            chans=chans,
            members=members,
            nobs=nobs,
            width=width,
        ),
        out_shape=[
            jax.ShapeDtypeStruct((members, 128), jnp.float32),
            jax.ShapeDtypeStruct((groups, bands, members, 128), jnp.float32),
        ],
        in_specs=[VMEM] * 5,
        out_specs=[VMEM] * 2,
        scratch_shapes=[
            pltpu.VMEM((members, 8, nobs), jnp.float32),
            pltpu.SemaphoreType.DMA((2, bands)),
            pltpu.SemaphoreType.DMA((2, groups)),
        ],
        compiler_params=pltpu.CompilerParams(
            vmem_limit_bytes=40 * 2**20, collective_id=1, has_side_effects=True
        ),
        name="grams",
    )(field, chan, col, obs_values, obs_prec)
    out = pl.pallas_call(
        functools.partial(analysis_kernel, members=members, chans=chans, real=real, width=width),
        out_shape=jax.ShapeDtypeStruct((members * real * 2 * height, 128), jnp.float32),
        in_specs=[SMEM, SMEM, VMEM, VMEM, VMEM],
        out_specs=VMEM,
        compiler_params=pltpu.CompilerParams(vmem_limit_bytes=40 * 2**20),
        name="analyse",
    )(neighbours, loc_weight, packed, gathered, field)
    out = out.reshape(members, real, width // 128, height, 128)
    return jnp.transpose(out, (0, 1, 3, 2, 4)).reshape(members, real, height, width)


def solution(mesh):
    placed = (
        P("grp", None, "band", None),
        P(),
        P(),
        P(),
        P(),
        P(("grp", "band"), None),
        P(("grp", "band"), None),
        P(("grp", "band"), None),
        P(("grp", "band"), None),
        P(("grp", "band"), None),
    )
    return jax.shard_map(
        on_device,
        mesh=mesh,
        in_specs=placed,
        out_specs=P(None, None, "band", "grp"),
        check_vma=False,
    )
```

```python
import functools

import jax
import jax.numpy as jnp
from jax import lax
from jax.experimental import pallas as pl
from jax.experimental.pallas import tpu as pltpu
from jax.sharding import PartitionSpec as P

NS_ITERS = 6
PAIR = 2
AHEAD = 3
ROWK = 224
SMEM = pl.BlockSpec(memory_space=pltpu.SMEM)
VMEM = pl.BlockSpec(memory_space=pltpu.VMEM)
MESH = pl.DeviceIdType.MESH
HIGH = lax.Precision.HIGHEST


def as_column(line):
    return jnp.transpose(jnp.broadcast_to(line, (8, line.shape[1])), (1, 0))[:, :1]


def forecast_kernel(
    own, w1, b1, w2, b2, field, near, far, ext, hidden, fore, stage, bias1, bias2, swap_sems, pass_sems, part_sems,
    *, chans, hid, lon, groups, bands
):
    grp, band = lax.axis_index("grp"), lax.axis_index("band")
    odd = lax.rem(band, 2)
    count = own.shape[0]
    width = lon // groups
    partner = band + 1 - 2 * odd
    target = band + 2 - 4 * odd
    origin = band - 2 + 4 * odd
    sends = (target >= 0) & (target < bands)
    receives = (origin >= 0) & (origin < bands)
    barrier = pltpu.get_barrier_semaphore()
    bias1[...] = as_column(b1[...])
    bias2[...] = as_column(b2[...])

    def greet(axis, peer):
        pl.semaphore_signal(barrier, inc=1, device_id={axis: peer}, device_id_type=MESH)

    greet("band", partner)
    for step in range(1, groups):
        greet("grp", jnp.bitwise_xor(grp, step))
    pl.when(receives)(lambda: greet("band", origin))

    @pl.when(jnp.logical_not(receives))
    def _():
        far[...] = jnp.zeros_like(far)

    pl.semaphore_wait(barrier, groups + sends.astype(jnp.int32))

    def swap(m):
        return pltpu.make_async_remote_copy(
            src_ref=own.at[m],
            dst_ref=near.at[m],
            send_sem=swap_sems.at[0, m],
            recv_sem=swap_sems.at[1, m],
            device_id={"band": partner},
            device_id_type=MESH,
        )

    def onward(m):
        return pltpu.make_async_remote_copy(
            src_ref=near.at[m],
            dst_ref=far.at[m],
            send_sem=pass_sems.at[0, m],
            recv_sem=pass_sems.at[1, m],
            device_id={"band": target},
            device_id_type=MESH,
        )

    def handout(pair, step):
        rows = pl.ds(pl.multiple_of((grp * count + pair * PAIR) * 8, 16), 8 * PAIR)
        return pltpu.make_async_remote_copy(
            src_ref=stage.at[pair, step],
            dst_ref=field.at[:, :, rows, :],
            send_sem=part_sems.at[0, pair, step],
            recv_sem=part_sems.at[1, pair, step],
            device_id={"grp": jnp.bitwise_xor(grp, step)},
            device_id_type=MESH,
        )

    for m in range(AHEAD):
        swap(m).start()
    swap(0).wait_recv()
    pl.when(sends)(lambda: onward(0).start())

    def one(pair, member):
        m = pair * PAIR + member

        @pl.when(m + 1 < count)
        def _():
            swap(m + 1).wait_recv()
            pl.when(sends)(lambda: onward(m + 1).start())

        @pl.when(m + AHEAD < count)
        def _():
            swap(m + AHEAD).start()

        pl.when(receives)(lambda: onward(m).wait_recv())

        for source, base in ((own, 2), (near, 4 * (1 - odd)), (far, 4 * odd)):
            for row in range(2):
                x = source[m, row].astype(jnp.float32)
                shifted = [
                    pltpu.roll(x, 1, 1),
                    x,
                    pltpu.roll(x, lon - 1, 1),
                    jnp.zeros((ROWK - 3 * chans, lon), jnp.float32),
                ]
                ext[base + row] = jnp.concatenate(shifted, axis=0).astype(jnp.bfloat16)

        for row in range(4):
            if row == 0:
                keep = band > 0
            elif row == 3:
                keep = band < bands - 1
            else:
                keep = None

            def tile(n, carry, row=row, keep=keep):
                cols = pl.ds(pl.multiple_of(n * 256, 256), 256)
                window = ext[row : row + 3, :, cols].reshape(3 * ROWK, 256)
                h = jnp.dot(w1[...], window, preferred_element_type=jnp.float32) + bias1[...]
                h = 0.5 * h
                h = h + h * jnp.tanh(h)
                if keep is not None:
                    h = jnp.where(keep, h, 0.0)
                hidden[row * hid : (row + 1) * hid, cols] = h.astype(jnp.bfloat16)
                return carry

            lax.fori_loop(0, lon // 256, tile, 0, unroll=4)

        for row in range(2):
            summed = jnp.dot(
                w2[...],
                hidden[row * hid : (row + 3) * hid, :],
                preferred_element_type=jnp.float32,
            )
            out = (
                pltpu.roll(summed[:chans], 1, 1)
                + summed[chans : 2 * chans]
                + pltpu.roll(summed[2 * chans :], lon - 1, 1)
                + own[m, row].astype(jnp.float32)
                + bias2[...]
            )
            for part in range(groups):
                piece = out[:, part * width : (part + 1) * width]
                fore[part, row, :, member * 8 : (member + 1) * 8, :] = piece.reshape(
                    chans // 8, 8, width
                )

    def both(pair, carry):
        for member in range(PAIR):
            one(pair, member)
        rows = pl.ds(pl.multiple_of((grp * count + pair * PAIR) * 8, 16), 8 * PAIR)
        for row in range(2):
            field[row, :, rows, :] = fore[grp, row].astype(jnp.bfloat16)
            for step in range(1, groups):
                stage[pair, step, row] = fore[jnp.bitwise_xor(grp, step), row].astype(jnp.bfloat16)
        for step in range(1, groups):
            handout(pair, step).start()
        return carry

    lax.fori_loop(0, count // PAIR, both, 0)

    def finish(pair, carry):
        for step in range(1, groups):
            handout(pair, step).wait()
        for member in range(PAIR):
            m = pair * PAIR + member
            swap(m).wait_send()
            pl.when(sends)(lambda m=m: onward(m).wait_send())
        return carry

    lax.fori_loop(0, count // PAIR, finish, 0)


def exchange_start(bands, groups):
    grp, band = lax.axis_index("grp"), lax.axis_index("band")
    barrier = pltpu.get_barrier_semaphore()
    for step in range(1, bands):
        peer = lax.rem(band + step, bands)
        pl.semaphore_signal(barrier, inc=1, device_id={"band": peer}, device_id_type=MESH)
    for step in range(1, groups):
        peer = jnp.bitwise_xor(grp, step)
        pl.semaphore_signal(barrier, inc=1, device_id={"grp": peer}, device_id_type=MESH)


def exchange_all(gathered, bands, groups, band_sems, grp_sems):
    grp, band = lax.axis_index("grp"), lax.axis_index("band")
    pl.semaphore_wait(pltpu.get_barrier_semaphore(), bands + groups - 2)
    first = [
        pltpu.make_async_remote_copy(
            src_ref=gathered.at[grp, band],
            dst_ref=gathered.at[grp, band],
            send_sem=band_sems.at[0, step],
            recv_sem=band_sems.at[1, step],
            device_id={"band": lax.rem(band + step, bands)},
            device_id_type=MESH,
        )
        for step in range(1, bands)
    ]
    for copy in first:
        copy.start()
    for copy in first:
        copy.wait()
    second = [
        pltpu.make_async_remote_copy(
            src_ref=gathered.at[grp],
            dst_ref=gathered.at[grp],
            send_sem=grp_sems.at[0, step],
            recv_sem=grp_sems.at[1, step],
            device_id={"grp": jnp.bitwise_xor(grp, step)},
            device_id_type=MESH,
        )
        for step in range(1, groups)
    ]
    for copy in second:
        copy.start()
    for copy in second:
        copy.wait()


def gram_kernel(
    field, index, obs, prec, packed, gathered, pred, band_sems, grp_sems,
    *, bands, groups, chans, members, nobs, width
):
    exchange_start(bands, groups)
    grp = lax.axis_index("grp")
    depth = chans * PAIR
    lane = lax.broadcasted_iota(jnp.int32, (nobs, depth), 1)
    lane_chan = (lane // 16) * 8 + lane % 8
    lane_member = (lane // 8) % 2
    col_iota = lax.broadcasted_iota(jnp.int32, (nobs, width), 1)
    ones = jnp.ones((8, width), jnp.bfloat16)
    packed[...] = jnp.zeros_like(packed)
    for row in range(2):
        place = as_column(index[row : row + 1, :].astype(jnp.float32)).astype(jnp.int32)
        pick_chan = lane_chan == lax.div(place, width)
        selects = [
            jnp.where(pick_chan & (lane_member == v), 1.0, 0.0).astype(jnp.bfloat16)
            for v in range(PAIR)
        ]
        pick_col = col_iota == lax.rem(place, width)

        for first in range(0, members, PAIR):
            values = field[row, :, first * 8 : (first + PAIR) * 8, :].reshape(depth, width)
            for v in range(PAIR):
                g = jnp.dot(selects[v], values, preferred_element_type=jnp.float32)
                g = jnp.where(pick_col, g, 0.0).astype(jnp.bfloat16)
                line = lax.dot_general(
                    ones, g, (((1,), (1,)), ((), ())), preferred_element_type=jnp.float32
                )
                pred[first + v] = line
        predicted = pred[:, 0, :]
        mean = jnp.sum(predicted, axis=0, keepdims=True) * (1.0 / members)
        perturb = predicted - mean
        innovation = obs[row : row + 1, :] - mean
        both = jnp.concatenate([perturb, jnp.broadcast_to(innovation, (8, nobs))], axis=0)
        packed[:, row * 64 : row * 64 + members + 8] = lax.dot_general(
            perturb * prec[row : row + 1, :],
            both,
            (((1,), (1,)), ((), ())),
            precision=HIGH,
            preferred_element_type=jnp.float32,
        )
    gathered[grp, lax.axis_index("band")] = packed[...]
    exchange_all(gathered, bands, groups, band_sems, grp_sems)


def analysis_kernel(neighbours, weights, mine, gathered, field, out, *, members, chans, real, width):
    eye = (
        lax.broadcasted_iota(jnp.int32, (members, members), 0)
        == lax.broadcasted_iota(jnp.int32, (members, members), 1)
    ).astype(jnp.float32)
    wide = members * 8
    expand = (
        lax.broadcasted_iota(jnp.int32, (wide, members), 0) // 8
        == lax.broadcasted_iota(jnp.int32, (wide, members), 1)
    ).astype(jnp.bfloat16)
    same = (
        lax.broadcasted_iota(jnp.int32, (wide, wide), 0) % 8
        == lax.broadcasted_iota(jnp.int32, (wide, wide), 1) % 8
    )

    def dot(a, b):
        return jnp.dot(a, b, precision=HIGH, preferred_element_type=jnp.float32)

    state = []
    for row in range(2):
        total = mine[...] if row == 0 else pltpu.roll(mine[...], 64, 1)
        for k in range(neighbours.shape[1]):
            j = neighbours[row, k]
            bands = gathered.shape[1]
            gram = gathered[j // (2 * bands), (j // 2) % bands]
            gram = jnp.where(j % 2 == 1, pltpu.roll(gram, 64, 1), gram)
            total = total + weights[row, k] * gram
        matrix = total[:, :members] + (members - 1.0) * eye
        norm = jnp.sqrt(jnp.sum(matrix * matrix, keepdims=True))
        state.append([matrix / norm, eye, total, norm])
    for sweep in range(NS_ITERS):
        halves = [1.5 * eye - 0.5 * dot(inv, root) for root, inv, _, _ in state]
        for entry, half in zip(state, halves):
            entry[0] = dot(entry[0], half)
            entry[1] = dot(half, entry[1])
    for row in range(2):
        _, inv, total, norm = state[row]
        mean_weight = dot(inv, dot(inv, total))[:, members : members + 1] / norm
        transform = (jnp.sqrt(members - 1.0) / jnp.sqrt(norm)) * inv + mean_weight
        transform = transform + (1.0 - jnp.sum(transform, axis=0, keepdims=True)) * (1.0 / members)
        spread = []
        for piece in range(3):
            part = transform.astype(jnp.bfloat16)
            transform = transform - part.astype(jnp.float32)
            tall = lax.dot_general(
                expand, part, (((1,), (1,)), ((), ())), preferred_element_type=jnp.float32
            ).astype(jnp.bfloat16)
            full = lax.dot_general(
                tall, expand, (((1,), (1,)), ((), ())), preferred_element_type=jnp.float32
            )
            spread.append(jnp.where(same, full, 0.0).astype(jnp.bfloat16))
        for block in range(chans // 8):
            x = field[row, block]
            y = jnp.dot(spread[0], x, preferred_element_type=jnp.float32)
            y = y + jnp.dot(spread[1], x, preferred_element_type=jnp.float32)
            y = y + jnp.dot(spread[2], x, preferred_element_type=jnp.float32)
            count = min(8, real - block * 8)
            for member in range(members):
                for half in range(width // 128):
                    start = (member * real + block * 8) * 4 + half * 2 + row
                    out[pl.ds(start, count, stride=4), :] = y[
                        member * 8 : member * 8 + count, half * 128 : (half + 1) * 128
                    ]


def on_device(
    prior_samples,
    conv1_weight,
    conv1_bias,
    conv2_weight,
    conv2_bias,
    obs_index,
    obs_values,
    obs_prec,
    neighbours,
    loc_weight,
):
    bands = lax.axis_size("band")
    groups = lax.axis_size("grp")
    own_members, real, height, lon = prior_samples.shape
    members = own_members * groups
    hid = conv1_weight.shape[2]
    width = lon // groups
    nobs = obs_index.shape[1]
    chans = -(-real // 8) * 8

    w1 = jnp.pad(conv1_weight, ((0, 0), (0, 0), (0, 0), (0, chans - real)))
    w1 = jnp.transpose(w1, (2, 0, 1, 3)).reshape(hid, 3, 3 * chans)
    w1 = jnp.pad(w1, ((0, 0), (0, 0), (0, ROWK - 3 * chans))).reshape(hid, 3 * ROWK)
    w2 = jnp.pad(conv2_weight, ((0, 0), (0, 0), (0, chans - real), (0, 0)))
    w2 = jnp.transpose(w2, (1, 2, 0, 3)).reshape(3 * chans, 3 * hid)
    b1 = conv1_bias[None, :]
    b2 = jnp.pad(conv2_bias, (0, chans - real))[None, :]

    pairs = own_members // PAIR
    blocks = chans // 8
    own = jnp.transpose(prior_samples, (0, 2, 1, 3))
    own = jnp.pad(own, ((0, 0), (0, 0), (0, chans - real), (0, 0)))
    halo = pltpu.VMEM((own_members, height, chans, lon), jnp.bfloat16)
    field = pl.pallas_call(
        functools.partial(
            forecast_kernel, chans=chans, hid=hid, lon=lon, groups=groups, bands=bands
        ),
        out_shape=jax.ShapeDtypeStruct((height, blocks, members * 8, width), jnp.bfloat16),
        in_specs=[VMEM] * 5,
        out_specs=VMEM,
        scratch_shapes=[
            halo,
            halo,
            pltpu.VMEM((6, ROWK, lon), jnp.bfloat16),
            pltpu.VMEM((4 * hid, lon), jnp.bfloat16),
            pltpu.VMEM((groups, height, blocks, 8 * PAIR, width), jnp.float32),
            pltpu.VMEM((pairs, groups, height, blocks, 8 * PAIR, width), jnp.bfloat16),
            pltpu.VMEM((hid, 1), jnp.float32),
            pltpu.VMEM((chans, 1), jnp.float32),
            pltpu.SemaphoreType.DMA((2, own_members)),
            pltpu.SemaphoreType.DMA((2, own_members)),
            pltpu.SemaphoreType.DMA((2, pairs, groups)),
        ],
        compiler_params=pltpu.CompilerParams(
            vmem_limit_bytes=44 * 2**20, collective_id=2, has_side_effects=True
        ),
        name="forecast",
    )(own, w1, b1, w2, b2)

    packed, gathered = pl.pallas_call(
        functools.partial(
            gram_kernel,
            bands=bands,
            groups=groups,
            chans=chans,
            members=members,
            nobs=nobs,
            width=width,
        ),
        out_shape=[
            jax.ShapeDtypeStruct((members, 128), jnp.float32),
            jax.ShapeDtypeStruct((groups, bands, members, 128), jnp.float32),
        ],
        in_specs=[VMEM] * 4,
        out_specs=[VMEM] * 2,
        scratch_shapes=[
            pltpu.VMEM((members, 8, nobs), jnp.float32),
            pltpu.SemaphoreType.DMA((2, bands)),
            pltpu.SemaphoreType.DMA((2, groups)),
        ],
        compiler_params=pltpu.CompilerParams(
            vmem_limit_bytes=40 * 2**20, collective_id=1, has_side_effects=True
        ),
        name="grams",
    )(field, obs_index, obs_values, obs_prec)
    out = pl.pallas_call(
        functools.partial(analysis_kernel, members=members, chans=chans, real=real, width=width),
        out_shape=jax.ShapeDtypeStruct((members * real * 2 * height, 128), jnp.float32),
        in_specs=[SMEM, SMEM, VMEM, VMEM, VMEM],
        out_specs=VMEM,
        compiler_params=pltpu.CompilerParams(vmem_limit_bytes=40 * 2**20),
        name="analyse",
    )(neighbours, loc_weight, packed, gathered, field)
    out = out.reshape(members, real, width // 128, height, 128)
    return jnp.transpose(out, (0, 1, 3, 2, 4)).reshape(members, real, height, width)


def solution(mesh):
    placed = (
        P("grp", None, "band", None),
        P(),
        P(),
        P(),
        P(),
        P(("grp", "band"), None),
        P(("grp", "band"), None),
        P(("grp", "band"), None),
        P(("grp", "band"), None),
        P(("grp", "band"), None),
    )
    return jax.shard_map(
        on_device,
        mesh=mesh,
        in_specs=placed,
        out_specs=P(None, None, "band", "grp"),
        check_vma=False,
    )
```

```python
import functools

import jax
import jax.numpy as jnp
from jax import lax
from jax.experimental import pallas as pl
from jax.experimental.pallas import tpu as pltpu
from jax.sharding import PartitionSpec as P

NS_ITERS = 6
PAIR = 2
AHEAD = 8
ROWK = 224
SMEM = pl.BlockSpec(memory_space=pltpu.SMEM)
VMEM = pl.BlockSpec(memory_space=pltpu.VMEM)
MESH = pl.DeviceIdType.MESH
HIGH = lax.Precision.HIGHEST


def as_column(line):
    return jnp.transpose(jnp.broadcast_to(line, (8, line.shape[1])), (1, 0))[:, :1]


def forecast_kernel(
    own, w1, b1, w2, b2, field, near, far, ext, hidden, fore, stage, bias1, bias2, swap_sems, pass_sems, part_sems,
    *, chans, hid, lon, groups, bands
):
    grp, band = lax.axis_index("grp"), lax.axis_index("band")
    odd = lax.rem(band, 2)
    count = own.shape[0]
    width = lon // groups
    partner = band + 1 - 2 * odd
    target = band + 2 - 4 * odd
    origin = band - 2 + 4 * odd
    sends = (target >= 0) & (target < bands)
    receives = (origin >= 0) & (origin < bands)
    barrier = pltpu.get_barrier_semaphore()
    bias1[...] = as_column(b1[...])
    bias2[...] = as_column(b2[...])

    def greet(axis, peer):
        pl.semaphore_signal(barrier, inc=1, device_id={axis: peer}, device_id_type=MESH)

    greet("band", partner)
    for step in range(1, groups):
        greet("grp", jnp.bitwise_xor(grp, step))
    pl.when(receives)(lambda: greet("band", origin))

    @pl.when(jnp.logical_not(receives))
    def _():
        far[...] = jnp.zeros_like(far)

    pl.semaphore_wait(barrier, groups + sends.astype(jnp.int32))

    def swap(m):
        return pltpu.make_async_remote_copy(
            src_ref=own.at[m],
            dst_ref=near.at[m],
            send_sem=swap_sems.at[0, m],
            recv_sem=swap_sems.at[1, m],
            device_id={"band": partner},
            device_id_type=MESH,
        )

    def onward(m):
        return pltpu.make_async_remote_copy(
            src_ref=near.at[m],
            dst_ref=far.at[m],
            send_sem=pass_sems.at[0, m],
            recv_sem=pass_sems.at[1, m],
            device_id={"band": target},
            device_id_type=MESH,
        )

    def handout(pair, step):
        rows = pl.ds(pl.multiple_of((grp * count + pair * PAIR) * 8, 16), 8 * PAIR)
        return pltpu.make_async_remote_copy(
            src_ref=stage.at[pair, step],
            dst_ref=field.at[:, :, rows, :],
            send_sem=part_sems.at[0, pair, step],
            recv_sem=part_sems.at[1, pair, step],
            device_id={"grp": jnp.bitwise_xor(grp, step)},
            device_id_type=MESH,
        )

    for m in range(min(AHEAD, count)):
        swap(m).start()
    swap(0).wait_recv()
    pl.when(sends)(lambda: onward(0).start())

    def one(pair, member):
        m = pair * PAIR + member

        @pl.when(m + 1 < count)
        def _():
            swap(m + 1).wait_recv()
            pl.when(sends)(lambda: onward(m + 1).start())

        @pl.when(m + AHEAD < count)
        def _():
            swap(m + AHEAD).start()

        pl.when(receives)(lambda: onward(m).wait_recv())

        for source, base in ((own, 2), (near, 4 * (1 - odd)), (far, 4 * odd)):
            for row in range(2):
                x = source[m, row].astype(jnp.float32)
                shifted = [
                    pltpu.roll(x, 1, 1),
                    x,
                    pltpu.roll(x, lon - 1, 1),
                    jnp.zeros((ROWK - 3 * chans, lon), jnp.float32),
                ]
                ext[base + row] = jnp.concatenate(shifted, axis=0).astype(jnp.bfloat16)

        for row in range(4):
            if row == 0:
                keep = band > 0
            elif row == 3:
                keep = band < bands - 1
            else:
                keep = None

            def tile(n, carry, row=row, keep=keep):
                cols = pl.ds(pl.multiple_of(n * 256, 256), 256)
                window = ext[row : row + 3, :, cols].reshape(3 * ROWK, 256)
                h = jnp.dot(w1[...], window, preferred_element_type=jnp.float32) + bias1[...]
                h = 0.5 * h
                h = h + h * jnp.tanh(h)
                if keep is not None:
                    h = jnp.where(keep, h, 0.0)
                hidden[row * hid : (row + 1) * hid, cols] = h.astype(jnp.bfloat16)
                return carry

            lax.fori_loop(0, lon // 256, tile, 0, unroll=4)

        for row in range(2):
            summed = jnp.dot(
                w2[...],
                hidden[row * hid : (row + 3) * hid, :],
                preferred_element_type=jnp.float32,
            )
            out = (
                pltpu.roll(summed[:chans], 1, 1)
                + summed[chans : 2 * chans]
                + pltpu.roll(summed[2 * chans :], lon - 1, 1)
                + own[m, row].astype(jnp.float32)
                + bias2[...]
            )
            for part in range(groups):
                piece = out[:, part * width : (part + 1) * width]
                fore[part, row, :, member * 8 : (member + 1) * 8, :] = piece.reshape(
                    chans // 8, 8, width
                )

    def both(pair, carry):
        for member in range(PAIR):
            one(pair, member)
        rows = pl.ds(pl.multiple_of((grp * count + pair * PAIR) * 8, 16), 8 * PAIR)
        for row in range(2):
            field[row, :, rows, :] = fore[grp, row].astype(jnp.bfloat16)
            for step in range(1, groups):
                stage[pair, step, row] = fore[jnp.bitwise_xor(grp, step), row].astype(jnp.bfloat16)
        for step in range(1, groups):
            handout(pair, step).start()
        return carry

    lax.fori_loop(0, count // PAIR, both, 0)

    def finish(pair, carry):
        for step in range(1, groups):
            handout(pair, step).wait()
        for member in range(PAIR):
            m = pair * PAIR + member
            swap(m).wait_send()
            pl.when(sends)(lambda m=m: onward(m).wait_send())
        return carry

    lax.fori_loop(0, count // PAIR, finish, 0)


def exchange_start(bands, groups):
    grp, band = lax.axis_index("grp"), lax.axis_index("band")
    barrier = pltpu.get_barrier_semaphore()
    for step in range(1, bands):
        peer = lax.rem(band + step, bands)
        pl.semaphore_signal(barrier, inc=1, device_id={"band": peer}, device_id_type=MESH)
    for step in range(1, groups):
        peer = jnp.bitwise_xor(grp, step)
        pl.semaphore_signal(barrier, inc=1, device_id={"grp": peer}, device_id_type=MESH)


def exchange_all(gathered, bands, groups, band_sems, grp_sems):
    grp, band = lax.axis_index("grp"), lax.axis_index("band")
    pl.semaphore_wait(pltpu.get_barrier_semaphore(), bands + groups - 2)
    first = [
        pltpu.make_async_remote_copy(
            src_ref=gathered.at[grp, band],
            dst_ref=gathered.at[grp, band],
            send_sem=band_sems.at[0, step],
            recv_sem=band_sems.at[1, step],
            device_id={"band": lax.rem(band + step, bands)},
            device_id_type=MESH,
        )
        for step in range(1, bands)
    ]
    for copy in first:
        copy.start()
    for copy in first:
        copy.wait()
    second = [
        pltpu.make_async_remote_copy(
            src_ref=gathered.at[grp],
            dst_ref=gathered.at[grp],
            send_sem=grp_sems.at[0, step],
            recv_sem=grp_sems.at[1, step],
            device_id={"grp": jnp.bitwise_xor(grp, step)},
            device_id_type=MESH,
        )
        for step in range(1, groups)
    ]
    for copy in second:
        copy.start()
    for copy in second:
        copy.wait()


def gram_kernel(
    field, index, obs, prec, packed, gathered, pred, band_sems, grp_sems,
    *, bands, groups, chans, members, nobs, width
):
    exchange_start(bands, groups)
    grp = lax.axis_index("grp")
    depth = chans * PAIR
    lane = lax.broadcasted_iota(jnp.int32, (nobs, depth), 1)
    lane_chan = (lane // 16) * 8 + lane % 8
    lane_member = (lane // 8) % 2
    col_iota = lax.broadcasted_iota(jnp.int32, (nobs, width), 1)
    ones = jnp.ones((8, width), jnp.bfloat16)
    packed[...] = jnp.zeros_like(packed)
    for row in range(2):
        place = as_column(index[row : row + 1, :].astype(jnp.float32)).astype(jnp.int32)
        pick_chan = lane_chan == lax.div(place, width)
        selects = [
            jnp.where(pick_chan & (lane_member == v), 1.0, 0.0).astype(jnp.bfloat16)
            for v in range(PAIR)
        ]
        pick_col = col_iota == lax.rem(place, width)

        for first in range(0, members, PAIR):
            values = field[row, :, first * 8 : (first + PAIR) * 8, :].reshape(depth, width)
            for v in range(PAIR):
                g = jnp.dot(selects[v], values, preferred_element_type=jnp.float32)
                g = jnp.where(pick_col, g, 0.0).astype(jnp.bfloat16)
                line = lax.dot_general(
                    ones, g, (((1,), (1,)), ((), ())), preferred_element_type=jnp.float32
                )
                pred[first + v] = line
        predicted = pred[:, 0, :]
        mean = jnp.sum(predicted, axis=0, keepdims=True) * (1.0 / members)
        perturb = predicted - mean
        innovation = obs[row : row + 1, :] - mean
        both = jnp.concatenate([perturb, jnp.broadcast_to(innovation, (8, nobs))], axis=0)
        packed[:, row * 64 : row * 64 + members + 8] = lax.dot_general(
            perturb * prec[row : row + 1, :],
            both,
            (((1,), (1,)), ((), ())),
            precision=HIGH,
            preferred_element_type=jnp.float32,
        )
    gathered[grp, lax.axis_index("band")] = packed[...]
    exchange_all(gathered, bands, groups, band_sems, grp_sems)


def analysis_kernel(neighbours, weights, mine, gathered, field, out, *, members, chans, real, width):
    eye = (
        lax.broadcasted_iota(jnp.int32, (members, members), 0)
        == lax.broadcasted_iota(jnp.int32, (members, members), 1)
    ).astype(jnp.float32)
    wide = members * 8
    expand = (
        lax.broadcasted_iota(jnp.int32, (wide, members), 0) // 8
        == lax.broadcasted_iota(jnp.int32, (wide, members), 1)
    ).astype(jnp.bfloat16)
    same = (
        lax.broadcasted_iota(jnp.int32, (wide, wide), 0) % 8
        == lax.broadcasted_iota(jnp.int32, (wide, wide), 1) % 8
    )

    def dot(a, b):
        return jnp.dot(a, b, precision=HIGH, preferred_element_type=jnp.float32)

    state = []
    for row in range(2):
        total = mine[...] if row == 0 else pltpu.roll(mine[...], 64, 1)
        for k in range(neighbours.shape[1]):
            j = neighbours[row, k]
            bands = gathered.shape[1]
            gram = gathered[j // (2 * bands), (j // 2) % bands]
            gram = jnp.where(j % 2 == 1, pltpu.roll(gram, 64, 1), gram)
            total = total + weights[row, k] * gram
        matrix = total[:, :members] + (members - 1.0) * eye
        norm = jnp.sqrt(jnp.sum(matrix * matrix, keepdims=True))
        state.append([matrix / norm, eye, total, norm])
    for sweep in range(NS_ITERS):
        halves = [1.5 * eye - 0.5 * dot(inv, root) for root, inv, _, _ in state]
        for entry, half in zip(state, halves):
            entry[0] = dot(entry[0], half)
            entry[1] = dot(half, entry[1])
    for row in range(2):
        _, inv, total, norm = state[row]
        mean_weight = dot(inv, dot(inv, total))[:, members : members + 1] / norm
        transform = (jnp.sqrt(members - 1.0) / jnp.sqrt(norm)) * inv + mean_weight
        transform = transform + (1.0 - jnp.sum(transform, axis=0, keepdims=True)) * (1.0 / members)
        spread = []
        for piece in range(3):
            part = transform.astype(jnp.bfloat16)
            transform = transform - part.astype(jnp.float32)
            tall = lax.dot_general(
                expand, part, (((1,), (1,)), ((), ())), preferred_element_type=jnp.float32
            ).astype(jnp.bfloat16)
            full = lax.dot_general(
                tall, expand, (((1,), (1,)), ((), ())), preferred_element_type=jnp.float32
            )
            spread.append(jnp.where(same, full, 0.0).astype(jnp.bfloat16))
        for block in range(chans // 8):
            x = field[row, block]
            y = jnp.dot(spread[0], x, preferred_element_type=jnp.float32)
            y = y + jnp.dot(spread[1], x, preferred_element_type=jnp.float32)
            y = y + jnp.dot(spread[2], x, preferred_element_type=jnp.float32)
            count = min(8, real - block * 8)
            for member in range(members):
                for half in range(width // 128):
                    start = (member * real + block * 8) * 4 + half * 2 + row
                    out[pl.ds(start, count, stride=4), :] = y[
                        member * 8 : member * 8 + count, half * 128 : (half + 1) * 128
                    ]


def on_device(
    prior_samples,
    conv1_weight,
    conv1_bias,
    conv2_weight,
    conv2_bias,
    obs_index,
    obs_values,
    obs_prec,
    neighbours,
    loc_weight,
):
    bands = lax.axis_size("band")
    groups = lax.axis_size("grp")
    own_members, real, height, lon = prior_samples.shape
    members = own_members * groups
    hid = conv1_weight.shape[2]
    width = lon // groups
    nobs = obs_index.shape[1]
    chans = -(-real // 8) * 8

    w1 = jnp.pad(conv1_weight, ((0, 0), (0, 0), (0, 0), (0, chans - real)))
    w1 = jnp.transpose(w1, (2, 0, 1, 3)).reshape(hid, 3, 3 * chans)
    w1 = jnp.pad(w1, ((0, 0), (0, 0), (0, ROWK - 3 * chans))).reshape(hid, 3 * ROWK)
    w2 = jnp.pad(conv2_weight, ((0, 0), (0, 0), (0, chans - real), (0, 0)))
    w2 = jnp.transpose(w2, (1, 2, 0, 3)).reshape(3 * chans, 3 * hid)
    b1 = conv1_bias[None, :]
    b2 = jnp.pad(conv2_bias, (0, chans - real))[None, :]

    pairs = own_members // PAIR
    blocks = chans // 8
    own = jnp.transpose(prior_samples, (0, 2, 1, 3))
    own = jnp.pad(own, ((0, 0), (0, 0), (0, chans - real), (0, 0)))
    halo = pltpu.VMEM((own_members, height, chans, lon), jnp.bfloat16)
    field = pl.pallas_call(
        functools.partial(
            forecast_kernel, chans=chans, hid=hid, lon=lon, groups=groups, bands=bands
        ),
        out_shape=jax.ShapeDtypeStruct((height, blocks, members * 8, width), jnp.bfloat16),
        in_specs=[VMEM] * 5,
        out_specs=VMEM,
        scratch_shapes=[
            halo,
            halo,
            pltpu.VMEM((6, ROWK, lon), jnp.bfloat16),
            pltpu.VMEM((4 * hid, lon), jnp.bfloat16),
            pltpu.VMEM((groups, height, blocks, 8 * PAIR, width), jnp.float32),
            pltpu.VMEM((pairs, groups, height, blocks, 8 * PAIR, width), jnp.bfloat16),
            pltpu.VMEM((hid, 1), jnp.float32),
            pltpu.VMEM((chans, 1), jnp.float32),
            pltpu.SemaphoreType.DMA((2, own_members)),
            pltpu.SemaphoreType.DMA((2, own_members)),
            pltpu.SemaphoreType.DMA((2, pairs, groups)),
        ],
        compiler_params=pltpu.CompilerParams(
            vmem_limit_bytes=44 * 2**20, collective_id=2, has_side_effects=True
        ),
        name="forecast",
    )(own, w1, b1, w2, b2)

    packed, gathered = pl.pallas_call(
        functools.partial(
            gram_kernel,
            bands=bands,
            groups=groups,
            chans=chans,
            members=members,
            nobs=nobs,
            width=width,
        ),
        out_shape=[
            jax.ShapeDtypeStruct((members, 128), jnp.float32),
            jax.ShapeDtypeStruct((groups, bands, members, 128), jnp.float32),
        ],
        in_specs=[VMEM] * 4,
        out_specs=[VMEM] * 2,
        scratch_shapes=[
            pltpu.VMEM((members, 8, nobs), jnp.float32),
            pltpu.SemaphoreType.DMA((2, bands)),
            pltpu.SemaphoreType.DMA((2, groups)),
        ],
        compiler_params=pltpu.CompilerParams(
            vmem_limit_bytes=40 * 2**20, collective_id=1, has_side_effects=True
        ),
        name="grams",
    )(field, obs_index, obs_values, obs_prec)
    out = pl.pallas_call(
        functools.partial(analysis_kernel, members=members, chans=chans, real=real, width=width),
        out_shape=jax.ShapeDtypeStruct((members * real * 2 * height, 128), jnp.float32),
        in_specs=[SMEM, SMEM, VMEM, VMEM, VMEM],
        out_specs=VMEM,
        compiler_params=pltpu.CompilerParams(vmem_limit_bytes=40 * 2**20),
        name="analyse",
    )(neighbours, loc_weight, packed, gathered, field)
    out = out.reshape(members, real, width // 128, height, 128)
    return jnp.transpose(out, (0, 1, 3, 2, 4)).reshape(members, real, height, width)


def solution(mesh):
    placed = (
        P("grp", None, "band", None),
        P(),
        P(),
        P(),
        P(),
        P(("grp", "band"), None),
        P(("grp", "band"), None),
        P(("grp", "band"), None),
        P(("grp", "band"), None),
        P(("grp", "band"), None),
    )
    return jax.shard_map(
        on_device,
        mesh=mesh,
        in_specs=placed,
        out_specs=P(None, None, "band", "grp"),
        check_vma=False,
    )
```
